512 devices in a mesh: seq: 32 (over x_hi, z, core), head: 16 (over y, x_lo).
Axes of the slice: x: 4 (x_hi: 2, x_lo: 2; x = x_hi * 2 + x_lo), y: 8, z: 8, core: 2. Of those that a mesh axis runs over, the one named last changes fastest.
Arguments:
- query: bfloat16 [32768, 2048], P(('seq', 'head')), may hold values from -6 to 6
- key: bfloat16 [32768, 2048], P(('seq', 'head')), may hold values from -6 to 6
- value: bfloat16 [32768, 2048], P(('seq', 'head')), may hold values from -6 to 6
- attn_out: bfloat16 [32768, 2048], P(('seq', 'head')), may hold values from -6 to 6
- grad_out: bfloat16 [32768, 2048], P(('seq', 'head')), may hold values from -96 to 96
- lse: float32 [16, 32768], P('head', 'seq'), may hold values from 7.5 to 9
- band: int32 [32, 5], replicated, may hold values from 0 to 1, as said below
Outputs:
- grad_query: bfloat16 [32768, 2048], P(('seq', 'head'))
- grad_key: bfloat16 [32768, 2048], P(('seq', 'head'))
- grad_value: bfloat16 [32768, 2048], P(('seq', 'head'))
The draws below stay inside these ranges and needn't reach their ends.
Inputs may be any that keep to these rules, and one draw needn't show every extreme that they name: `band`: column 2 (the block itself) is always 1; entries whose key block lies outside the video are 0; some block lists all 5 key blocks.
All inputs are finite; a program needn't handle non-finite values.
Results may differ from the reference program's by a relative error of at most 0.0055.
Values may be sent and summed in bfloat16 or wider, within the bound.
A program may use at most 64 MiB of HBM per device.

```python
import math
import jax
import jax.numpy as jnp
from jax import lax

HD = 128
BLK = 1024
R = 2
HEADS = 16
NBLK = 32
SEQ = 32768


def draw_band(key, part):
    key = jax.random.fold_in(key, 7)
    picked = jax.random.randint(key, (NBLK, 2 * R + 1), 0, 2)
    rows = jnp.arange(NBLK, dtype=jnp.int32)[:, None]
    columns = jnp.arange(2 * R + 1, dtype=jnp.int32)[None, :]
    target = rows + columns - R
    inside = (target >= 0) & (target < NBLK)
    full_row = jax.random.randint(jax.random.fold_in(key, 5), (), R, NBLK - R)
    listed = jnp.where((columns == R) | (rows == full_row), 1, picked)
    return jnp.where(inside, listed, 0).astype(jnp.int32)


def levels(own_key, dims, pieces, least, high):
    gain = 1.0
    for dim, parts in pieces:
        steps = jax.random.uniform(jax.random.fold_in(jax.random.fold_in(own_key, 6), dim), (parts,), jnp.float32, least / len(pieces), high / len(pieces))
        gain = gain * jnp.repeat(jnp.exp(steps), dims[dim] // parts).reshape((-1,) + (1,) * (len(dims) - 1 - dim))
    return gain


def gaussian(stream_key, shape, spread, bound, pieces=(), kind=jnp.bfloat16):
    loudness = levels(stream_key, shape, pieces, -0.22, 0.18) if pieces else 1.0
    drawn = jax.random.normal(stream_key, shape, jnp.float32) * spread * loudness
    return jnp.minimum(jnp.maximum(drawn, -bound), bound).astype(kind)


def setup_inputs(seed: int = 0) -> dict:
    streams_of = jax.random.split(jax.random.key(seed), 8)
    query = gaussian(streams_of[0], (SEQ, HEADS * HD), 1.0, 6.0, ((0, 512),))
    key = gaussian(streams_of[1], (SEQ, HEADS * HD), 1.0, 6.0, ((0, 512),))
    value = gaussian(streams_of[2], (SEQ, HEADS * HD), 1.0, 6.0, ((0, 512),))
    attn_out = gaussian(streams_of[3], (SEQ, HEADS * HD), 1.0, 6.0, ((0, 512),))
    grad_out = gaussian(streams_of[4], (SEQ, HEADS * HD), 16.0, 96.0, ((0, 512),))
    lse = jnp.clip(7.5 + 1.5 * jax.random.uniform(streams_of[5], (HEADS, SEQ), jnp.float32) ** levels(streams_of[5], (HEADS, SEQ), ((0, 16), (1, 32)), -0.2, 0.2), 7.5, 9.0)
    band = draw_band(jax.random.fold_in(streams_of[7], 71), 0)
    return dict(query=query, key=key, value=value, attn_out=attn_out, grad_out=grad_out, lse=lse, band=band)


def pair_grads(query_blk, grad_blk, lse_row, delta_row, key_blk, value_blk):
    scale = 1.0 / math.sqrt(query_blk.shape[1])
    scores = jnp.dot(query_blk, key_blk.T, preferred_element_type=jnp.float32) * scale
    probs = jnp.exp(scores - lse_row[:, None])
    probs_low = probs.astype(jnp.bfloat16)
    grad_value = jnp.dot(probs_low.T, grad_blk, preferred_element_type=jnp.float32)
    grad_prob = jnp.dot(grad_blk, value_blk.T, preferred_element_type=jnp.float32)
    grad_score = (probs * (grad_prob - delta_row[:, None]) * scale).astype(jnp.bfloat16)
    grad_query = jnp.dot(grad_score, key_blk, preferred_element_type=jnp.float32)
    grad_key = jnp.dot(grad_score.T, query_blk, preferred_element_type=jnp.float32)
    return (grad_query, grad_key, grad_value)

def rounded(term):
    return lax.optimization_barrier(term.astype(jnp.bfloat16)).astype(jnp.float32)

def reference(query, key, value, attn_out, grad_out, lse, band):
    product = grad_out.astype(jnp.float32) * attn_out.astype(jnp.float32)
    delta = lax.optimization_barrier(jnp.sum(product.reshape(SEQ, HEADS, HD), axis=2))

    def one_head(head):
        start_col = (head * HD).astype(jnp.int32)
        query_h = lax.dynamic_slice_in_dim(query, start_col, HD, 1)
        key_h = lax.dynamic_slice_in_dim(key, start_col, HD, 1)
        value_h = lax.dynamic_slice_in_dim(value, start_col, HD, 1)
        grad_h = lax.dynamic_slice_in_dim(grad_out, start_col, HD, 1)
        lse_h = lax.dynamic_index_in_dim(lse, head, 0, keepdims=False)
        delta_h = lax.dynamic_index_in_dim(delta, head, 1, keepdims=False)
        zeros = jnp.zeros((SEQ, HD), jnp.float32)

        def per_block(block, carry):
            block = jnp.asarray(block).astype(jnp.int32)
            start = (block * BLK).astype(jnp.int32)
            query_blk = lax.dynamic_slice_in_dim(query_h, start, BLK, 0)
            grad_blk = lax.dynamic_slice_in_dim(grad_h, start, BLK, 0)
            lse_row = lax.dynamic_slice_in_dim(lse_h, start, BLK, 0)
            delta_row = lax.dynamic_slice_in_dim(delta_h, start, BLK, 0)
            for column in range(2 * R + 1):
                target = jnp.clip(block + column - R, 0, NBLK - 1).astype(jnp.int32)
                kstart = (target * BLK).astype(jnp.int32)
                key_blk = lax.dynamic_slice_in_dim(key_h, kstart, BLK, 0)
                value_blk = lax.dynamic_slice_in_dim(value_h, kstart, BLK, 0)

                def active(state, kstart=kstart, key_blk=key_blk, value_blk=value_blk, column=column):
                    acc_query, acc_key, acc_value = state
                    part_query, part_key, part_value = pair_grads(query_blk, grad_blk, lse_row, delta_row, key_blk, value_blk)
                    if column != R:
                        part_key = rounded(part_key)
                        part_value = rounded(part_value)
                    acc_query = lax.dynamic_update_slice_in_dim(acc_query, lax.dynamic_slice_in_dim(acc_query, start, BLK, 0) + part_query, start, 0)
                    acc_key = lax.dynamic_update_slice_in_dim(acc_key, lax.dynamic_slice_in_dim(acc_key, kstart, BLK, 0) + part_key, kstart, 0)
                    acc_value = lax.dynamic_update_slice_in_dim(acc_value, lax.dynamic_slice_in_dim(acc_value, kstart, BLK, 0) + part_value, kstart, 0)
                    return (acc_query, acc_key, acc_value)

                def passive(state):
                    return state
                carry = lax.cond(band[block, column] == 1, active, passive, carry)
            return carry
        acc_query, acc_key, acc_value = lax.fori_loop(0, NBLK, per_block, (zeros, zeros, zeros))
        return (acc_query.astype(jnp.bfloat16), acc_key.astype(jnp.bfloat16), acc_value.astype(jnp.bfloat16))
    stacked = lax.map(one_head, jnp.arange(HEADS, dtype=jnp.int32))

    def arrange(block):
        return jnp.transpose(block, (1, 0, 2)).reshape(SEQ, HEADS * HD)
    return (arrange(stacked[0]), arrange(stacked[1]), arrange(stacked[2]))
```

```python
import math

import jax
import jax.numpy as jnp
from jax import lax
from jax.experimental import pallas as pl
from jax.experimental.pallas import tpu as pltpu
from jax.sharding import PartitionSpec as P

R = 2
HD = 128
SLOTS = 2 * R
LOG2E = 1.4426950408889634
SCALE = 1.0 / math.sqrt(HD)
UNLISTED = 1e30
MESH = pl.DeviceIdType.MESH
NT = (((1,), (1,)), ((), ()))
NN = (((1,), (0,)), ((), ()))


def dot(a, b, dims):
    return lax.dot_general(a, b, dims, preferred_element_type=jnp.float32)


def slot_step(slot, sign):
    return sign * (1 + slot // 2) * (1 - 2 * ((slot * (3 - slot)) // 2))


def far_slot(slot):
    return jnp.where(slot < 2, slot, 5 - slot)


def kernel(
    nseq,
    nhead,
    query,
    key,
    value,
    attn_out,
    grad_out,
    lse,
    band,
    out_query,
    out_key,
    out_value,
    own_qg,
    own_kv,
    far_qg,
    own_rows,
    far_rows,
    delta_out,
    delta_in,
    key_t,
    acc_query,
    acc_key,
    acc_value,
    term_out,
    term_in,
    res_query,
    res_kv,
    qg_send,
    qg_recv,
    kv_send,
    kv_recv,
    delta_send,
    delta_recv,
    far_send,
    far_recv,
    rows_send,
    rows_recv,
    term_send,
    term_recv,
    res_send,
    res_recv,
):
    here = lax.axis_index("seq")
    head = lax.axis_index("head")
    sign = 1 - 2 * lax.rem(here, 2)
    rows = query.shape[0]
    block = rows * nhead

    def cols(which):
        return pl.ds(pl.multiple_of(which * HD, HD), HD)

    def part(which):
        return pl.ds(pl.multiple_of(which * rows, rows), rows)

    def peer(step):
        return lax.rem(head + step, nhead)

    def neighbour(slot):
        other = here + slot_step(slot, sign)
        return other, jnp.logical_and(other >= 0, other < nseq)

    def remote(src, dst, send, recv, **where):
        return pltpu.make_async_remote_copy(
            src_ref=src, dst_ref=dst, send_sem=send, recv_sem=recv,
            device_id=where, device_id_type=MESH,
        )

    def drain(ref, sem):
        pltpu.make_async_copy(ref, ref, sem).wait()

    barrier = pltpu.get_barrier_semaphore()

    def greet(step, carry):
        pl.semaphore_signal(barrier, inc=1, device_id={"head": peer(step)}, device_id_type=MESH)
        return carry

    lax.fori_loop(1, nhead, greet, 0)
    for slot in range(SLOTS):
        other, inside = neighbour(slot)

        @pl.when(inside)
        def _(other=other):
            pl.semaphore_signal(barrier, inc=1, device_id={"seq": other}, device_id_type=MESH)

    count = nhead - 1
    for slot in range(SLOTS):
        count = count + jnp.where(neighbour(slot)[1], 1, 0)
    pl.semaphore_wait(barrier, count)

    def send_qg(step, carry):
        to = peer(step)
        remote(query.at[:, cols(to)], own_qg.at[0, part(head), :], qg_send, qg_recv, head=to).start()
        remote(grad_out.at[:, cols(to)], own_qg.at[1, part(head), :], qg_send, qg_recv, head=to).start()
        return carry

    lax.fori_loop(1, nhead, send_qg, 0)
    pltpu.make_async_copy(query.at[:, cols(head)], own_qg.at[0, part(head), :], qg_recv).start()
    pltpu.make_async_copy(grad_out.at[:, cols(head)], own_qg.at[1, part(head), :], qg_recv).start()

    lane = lax.broadcasted_iota(jnp.int32, (rows, HD), 1)
    sums = jnp.zeros((rows, HD), jnp.float32)
    for which in range(nhead):
        at = slice(which * HD, (which + 1) * HD)
        product = grad_out[:, at].astype(jnp.float32) * attn_out[:, at].astype(jnp.float32)
        sums = jnp.where(lane == which, jnp.sum(product, axis=1, keepdims=True), sums)
    across = jnp.concatenate([sums, sums], axis=0).T
    half = lax.broadcasted_iota(jnp.int32, (1, HD), 1) // rows
    across = jnp.where(half == lax.rem(head, 2), across, 0.0)
    for which in range(nhead):
        delta_out[which] = across[which : which + 1, :]

    def send_delta(step, carry):
        to = peer(step)
        remote(delta_out.at[to], delta_in.at[head], delta_send, delta_recv, head=to).start()
        return carry

    lax.fori_loop(1, nhead, send_delta, 0)
    pltpu.make_async_copy(delta_out.at[head], delta_in.at[head], delta_recv).start()

    def send_kv(step, carry):
        to = peer(step)
        remote(key.at[:, cols(to)], own_kv.at[0, part(head), :], kv_send, kv_recv, head=to).start()
        remote(value.at[:, cols(to)], own_kv.at[1, part(head), :], kv_send, kv_recv, head=to).start()
        return carry

    lax.fori_loop(1, nhead, send_kv, 0)
    pltpu.make_async_copy(key.at[:, cols(head)], own_kv.at[0, part(head), :], kv_recv).start()
    pltpu.make_async_copy(value.at[:, cols(head)], own_kv.at[1, part(head), :], kv_recv).start()

    drain(delta_in, delta_recv)
    own_rows[0:1, :] = lse[...] * LOG2E + math.log2(1.0 / SCALE)
    for pair in range(block // HD):
        own_rows[1:2, pair * HD : (pair + 1) * HD] = delta_in[2 * pair] + delta_in[2 * pair + 1]
    drain(own_qg, qg_recv)

    for slot in range(SLOTS):
        other, inside = neighbour(slot)

        @pl.when(inside)
        def _(slot=slot, other=other):
            there = slot if slot < 2 else 5 - slot
            remote(own_qg, far_qg.at[there], far_send.at[slot], far_recv.at[there], seq=other).start()
            remote(own_rows, far_rows.at[there], rows_send.at[slot], rows_recv.at[there], seq=other).start()

    acc_query[...] = jnp.zeros_like(acc_query)
    acc_key[...] = jnp.zeros_like(acc_key)
    acc_value[...] = jnp.zeros_like(acc_value)
    drain(own_kv, kv_recv)
    key_t[...] = own_kv[0].T
    chunk = min(256, block)

    def pair_grads(qg, shift, delta):
        def step(index, carry):
            at = pl.ds(pl.multiple_of(index * chunk, chunk), chunk)
            query_rows = qg[0]
            grad_rows = qg[1]
            scores = dot(own_kv[0, at, :], query_rows, NT)
            probs = jnp.exp2(scores * (SCALE * LOG2E) - shift)
            grad_prob = dot(own_kv[1, at, :], grad_rows, NT)
            probs_low = probs.astype(jnp.bfloat16)
            grad_score = (probs * (grad_prob - delta)).astype(jnp.bfloat16)
            acc_value[at, :] += dot(probs_low, grad_rows, NN)
            acc_key[at, :] += dot(grad_score, query_rows, NN)
            acc_query[...] += dot(key_t[:, at], grad_score, NN)
            return carry

        lax.fori_loop(0, block // chunk, step, 0)

    def far_pair(slot, carry):
        other, inside = neighbour(slot)

        @pl.when(inside)
        def _():
            there = far_slot(slot)
            drain(far_rows.at[slot], rows_recv.at[slot])
            drain(far_qg.at[slot], far_recv.at[slot])
            listed = band[other, here - other + R] == 1
            shift = jnp.where(listed, far_rows[slot, 0:1, :], UNLISTED)
            pair_grads(far_qg.at[slot], shift, far_rows[slot, 1:2, :])
            term_out[slot] = acc_query[...].astype(jnp.bfloat16)
            acc_query[...] = jnp.zeros_like(acc_query)
            remote(term_out.at[slot], term_in.at[there], term_send.at[slot], term_recv.at[there], seq=other).start()

        return carry

    lax.fori_loop(0, SLOTS, far_pair, 0)
    pair_grads(own_qg, own_rows[0:1, :], own_rows[1:2, :])

    def send_result(src, out, which):
        def step(index, carry):
            to = peer(index)
            remote(src.at[part(to), :], out.at[:, cols(head)], res_send.at[which], res_recv.at[which], head=to).start()
            return carry

        lax.fori_loop(1, nhead, step, 0)
        pltpu.make_async_copy(src.at[part(head), :], out.at[:, cols(head)], res_recv.at[which]).start()

    res_kv[0] = acc_key[...].astype(jnp.bfloat16)
    send_result(res_kv.at[0], out_key, 1)
    res_kv[1] = (acc_value[...] * (1.0 / SCALE)).astype(jnp.bfloat16)
    send_result(res_kv.at[1], out_value, 2)

    for slot in range(SLOTS):
        other, inside = neighbour(slot)

        @pl.when(inside)
        def _(slot=slot):
            drain(term_in.at[slot], term_recv.at[slot])
            acc_query[...] += term_in[slot].astype(jnp.float32)

    res_query[...] = acc_query[...].T.astype(jnp.bfloat16)
    send_result(res_query, out_query, 0)

    sent = pl.ds(0, (nhead - 1) * rows)
    drain(own_qg.at[:, sent, :], qg_send)
    drain(own_kv.at[:, sent, :], kv_send)
    drain(delta_in.at[pl.ds(0, nhead - 1)], delta_send)
    for slot in range(SLOTS):

        @pl.when(neighbour(slot)[1])
        def _(slot=slot):
            drain(own_qg, far_send.at[slot])
            drain(own_rows, rows_send.at[slot])
            drain(term_out.at[slot], term_send.at[slot])

    for which in range(3):
        drain(res_query.at[sent, :], res_send.at[which])
    drain(out_key, res_recv.at[1])
    drain(out_value, res_recv.at[2])
    drain(out_query, res_recv.at[0])


def per_device(query, key, value, attn_out, grad_out, lse, band):
    nseq, nhead = lax.axis_size("seq"), lax.axis_size("head")
    rows, width = query.shape
    block = rows * nhead
    low, full = jnp.bfloat16, jnp.float32
    vmem = pl.BlockSpec(memory_space=pltpu.VMEM)
    result = jax.ShapeDtypeStruct((rows, width), low)
    dma = pltpu.SemaphoreType.DMA

    def body(*refs):
        kernel(nseq, nhead, *refs)

    return pl.pallas_call(
        body,
        out_shape=(result,) * 3,
        in_specs=[vmem] * 6 + [pl.BlockSpec(memory_space=pltpu.SMEM)],
        out_specs=[vmem] * 3,
        scratch_shapes=[
            pltpu.VMEM((2, block, HD), low),
            pltpu.VMEM((2, block, HD), low),
            pltpu.VMEM((SLOTS, 2, block, HD), low),
            pltpu.VMEM((2, block), full),
            pltpu.VMEM((SLOTS, 2, block), full),
            pltpu.VMEM((nhead, 1, HD), full),
            pltpu.VMEM((nhead, 1, HD), full),
            pltpu.VMEM((HD, block), low),
            pltpu.VMEM((HD, block), full),
            pltpu.VMEM((block, HD), full),
            pltpu.VMEM((block, HD), full),
            pltpu.VMEM((SLOTS, HD, block), low),
            pltpu.VMEM((SLOTS, HD, block), low),
            pltpu.VMEM((block, HD), low),
            pltpu.VMEM((2, block, HD), low),
            dma, dma, dma, dma, dma, dma,
            dma((SLOTS,)), dma((SLOTS,)),
            dma((SLOTS,)), dma((SLOTS,)),
            dma((SLOTS,)), dma((SLOTS,)),
            dma((3,)), dma((3,)),
        ],
        compiler_params=pltpu.CompilerParams(
            collective_id=0, has_side_effects=True, vmem_limit_bytes=48 * 2**20
        ),
        cost_estimate=pl.CostEstimate(
            flops=25 * 2 * block * block * HD, bytes_accessed=8 * rows * width * 2,
            transcendentals=5 * block * block,
        ),
        name="attention_grads",
    )(query, key, value, attn_out, grad_out, lse, band)


def solution(mesh):
    rows = P(("seq", "head"), None)
    return jax.shard_map(
        per_device, mesh=mesh, in_specs=(rows,) * 5 + (P("head", "seq"), P()),
        out_specs=(rows,) * 3, check_vma=False,
    )
```

```python
import math

import jax
import jax.numpy as jnp
from jax import lax
from jax.experimental import pallas as pl
from jax.experimental.pallas import tpu as pltpu
from jax.sharding import PartitionSpec as P

R = 2
HD = 128
SLOTS = 2 * R
OWN = SLOTS
PARTS = 4
FIRST = 4
AFTER = ((1, (4,)), (2, (5,)), (3, (6,)))
NEAR = 1
LOG2E = 1.4426950408889634
SCALE = 1.0 / math.sqrt(HD)
UNLISTED = 1e30
MESH = pl.DeviceIdType.MESH
NT = (((1,), (1,)), ((), ()))
NN = (((1,), (0,)), ((), ()))


def dot(a, b, dims):
    return lax.dot_general(a, b, dims, preferred_element_type=jnp.float32)


def slot_step(slot, sign):
    return sign * (1 + slot // 2) * (1 - 2 * ((slot * (3 - slot)) // 2))


def far_slot(slot):
    return jnp.where(slot < 2, slot, 5 - slot)


def kernel(
    nseq,
    nhead,
    query_hbm,
    key_hbm,
    value_hbm,
    attn_out_hbm,
    grad_out_hbm,
    lse_hbm,
    band,
    out_query,
    out_key,
    out_value,
    query,
    key,
    value,
    attn_out,
    grad_out,
    lse,
    lse_rows,
    across,
    qg,
    kv,
    rows_of,
    delta_out,
    delta_in,
    key_t,
    acc_query,
    acc_part,
    acc_key,
    acc_value,
    term_out,
    term_in,
    res_query,
    res_kv,
    load_sem,
    qg_send,
    qg_recv,
    kv_send,
    kv_recv,
    delta_send,
    delta_recv,
    far_send,
    far_recv,
    rows_send,
    rows_recv,
    term_send,
    term_recv,
    res_send,
    res_recv,
    ready,
):
    here = lax.axis_index("seq")
    head = lax.axis_index("head")
    sign = 1 - 2 * lax.rem(here, 2)
    row = nseq // 2 if nseq >= 8 * R else nseq
    place_in_row = lax.rem(here, row)
    rows = query.shape[0]
    block = rows * nhead
    chunk = block // PARTS
    per = nhead // PARTS
    ny = nhead // 2

    def cols(which):
        return pl.ds(pl.multiple_of(which * HD, HD), HD)

    def part(which):
        return pl.ds(pl.multiple_of(which * rows, rows), rows)

    def quarter(which):
        return pl.ds(pl.multiple_of(which * chunk, chunk), chunk)

    def offset(place):
        if ny != 8:
            return place // 2, place % 2
        group, which = place // 4, place % 4
        reach = jnp.where(group == 3, 2, 1 + 2 * (which // 2))
        along_y = jnp.where(which % 2 == 1, ny - reach, reach)
        along_y = jnp.where(group == 0, 4 * (which // 2), along_y)
        along_x = jnp.where(group == 0, which % 2, jnp.where(group == 3, which // 2, group - 1))
        return along_y, along_x

    def sender(place):
        along_y, along_x = offset(place)
        return 2 * lax.rem(head // 2 + ny - along_y, ny) + lax.rem(head + along_x, 2)

    def receiver(place):
        along_y, along_x = offset(place)
        return 2 * lax.rem(head // 2 + along_y, ny) + lax.rem(head + along_x, 2)

    def after(step):
        return lax.rem(head + step, nhead)

    def neighbour(slot):
        other = here + slot_step(slot, sign)
        return other, jnp.logical_and(other >= 0, other < nseq)

    def standing(slot):
        other, inside = neighbour(slot)
        ahead = lax.rem(other + nseq, row) - place_in_row
        later = jnp.logical_and(inside, ahead > 0)
        earlier = jnp.logical_and(inside, ahead < 0)
        return other, later, earlier, jnp.logical_and(inside, ahead > R)

    def ordered(turn):
        last = jnp.where(turn < 3, lax.rem(turn + 1, 3), turn)
        slot = jnp.where(place_in_row == 0, lax.rem(SLOTS - turn, SLOTS), turn)
        slot = jnp.where(place_in_row == row - 1, last, slot)
        return jnp.where(place_in_row == row - 2, lax.rem(turn + 3, SLOTS), slot)

    def remote(src, dst, send, recv, **where):
        return pltpu.make_async_remote_copy(
            src_ref=src, dst_ref=dst, send_sem=send, recv_sem=recv,
            device_id=where, device_id_type=MESH,
        )

    def drain(ref, sem):
        pltpu.make_async_copy(ref, ref, sem).wait()

    loads = [
        pltpu.make_async_copy(src, dst, load_sem.at[at])
        for at, (src, dst) in enumerate(
            (
                (query_hbm, query),
                (grad_out_hbm, grad_out),
                (attn_out_hbm, attn_out),
                (key_hbm, key),
                (value_hbm, value),
                (lse_hbm, lse),
            )
        )
    ]
    for load in loads:
        load.start()

    barrier = pltpu.get_barrier_semaphore()

    def greet(step, carry):
        pl.semaphore_signal(barrier, inc=1, device_id={"head": after(step)}, device_id_type=MESH)
        return carry

    lax.fori_loop(1, nhead, greet, 0)
    count = nhead - 1
    for slot in range(SLOTS):
        other, later, earlier, _ = standing(slot)
        count = count + jnp.where(earlier, 1, 0)

        @pl.when(later)
        def _(other=other):
            pl.semaphore_signal(barrier, inc=1, device_id={"seq": other}, device_id_type=MESH)

    pl.semaphore_wait(barrier, count)
    for slot in range(SLOTS):
        other, _, earlier, _ = standing(slot)

        @pl.when(earlier)
        def _(slot=slot, other=other):
            there = slot if slot < 2 else 5 - slot
            pl.semaphore_signal(ready.at[there], inc=1, device_id={"seq": other}, device_id_type=MESH)

    def exchange(first, second, dst, send, recv, index):
        def step(place, carry):
            to = receiver(place)

            @pl.when(place > 0)
            def _():
                remote(first.at[:, cols(to)], dst.at[0, part(place), :], send, recv.at[index], head=to).start()
                remote(second.at[:, cols(to)], dst.at[1, part(place), :], send, recv.at[index], head=to).start()

            return carry

        lax.fori_loop(index * per, index * per + per, step, 0)

    def packet(number):
        if number < PARTS:
            exchange(query, grad_out, qg.at[OWN], qg_send, qg_recv, number)
        else:
            exchange(key, value, kv, kv_send, kv_recv, number - PARTS)

    for load in loads[:2] + loads[3:5]:
        load.wait()
    for number in range(FIRST):
        packet(number)
    for at, (first, second) in enumerate(((query, grad_out), (key, value))):
        dst, recv = ((qg.at[OWN], qg_recv), (kv, kv_recv))[at]
        pltpu.make_async_copy(first.at[:, cols(head)], dst.at[0, part(0), :], recv.at[0]).start()
        pltpu.make_async_copy(second.at[:, cols(head)], dst.at[1, part(0), :], recv.at[0]).start()

    loads[2].wait()
    lane = lax.broadcasted_iota(jnp.int32, (rows, HD), 1)
    sums = jnp.zeros((rows, HD), jnp.float32)
    for which in range(nhead):
        at = slice(which * HD, (which + 1) * HD)
        product = grad_out[:, at].astype(jnp.float32) * attn_out[:, at].astype(jnp.float32)
        sums = jnp.where(lane == which, jnp.sum(product, axis=1, keepdims=True), sums)
    across[...] = jnp.concatenate([sums, sums], axis=0).T
    low_half = lax.broadcasted_iota(jnp.int32, (1, HD), 1) < rows
    for place in range(nhead):
        to = receiver(place)
        mine = low_half if place % 2 == 0 else jnp.logical_not(low_half)
        delta_out[place] = jnp.where(mine, across[pl.ds(to, 1), :], 0.0)
        if place:
            remote(delta_out.at[place], delta_in.at[place], delta_send, delta_recv, head=to).start()
        else:
            pltpu.make_async_copy(delta_out.at[0], delta_in.at[0], delta_recv).start()

    loads[5].wait()
    lanes = block // HD
    for at in range(lanes):
        lse_rows[at : at + 1, :] = lse[:, at * HD : (at + 1) * HD]

    def lse_half(place):
        source = sender(place)
        one = lse_rows[pl.ds(source // 2, 1), :]
        other = jnp.concatenate([one[:, rows:], one[:, :rows]], axis=1)
        return jnp.where(lax.rem(source, 2) == place % 2, one, other)

    for at in range(lanes):
        turned = jnp.where(low_half, lse_half(2 * at), lse_half(2 * at + 1))
        rows_of[OWN, 0:1, at * HD : (at + 1) * HD] = turned * LOG2E + math.log2(1.0 / SCALE)
    acc_query[...] = jnp.zeros_like(acc_query)
    acc_key[...] = jnp.zeros_like(acc_key)
    acc_value[...] = jnp.zeros_like(acc_value)

    def forward_piece(slot, index, other):
        there = slot if slot < 2 else 5 - slot
        at = quarter(index)
        remote(
            qg.at[OWN, :, at, :], qg.at[there, :, at, :],
            far_send.at[slot, index], far_recv.at[there, index], seq=other,
        ).start()

    def forward(index, carry):
        drain(qg.at[OWN, :, quarter(index), :], qg_recv.at[index])
        for slot in range(SLOTS):
            other, later, earlier, late = standing(slot)
            prompt = jnp.logical_and(later, jnp.logical_not(late))
            @pl.when(prompt)
            def _(slot=slot, other=other):
                @pl.when(index == 0)
                def _():
                    pl.semaphore_wait(ready.at[slot], 1)

                if slot != 2:
                    forward_piece(slot, index, other)

            @pl.when(jnp.logical_and(earlier, slot != 2))
            def _(slot=slot, other=other):
                forward_piece(slot, index, other)

        for moment, numbers in AFTER:

            @pl.when(index == moment)
            def _(numbers=numbers):
                for number in numbers:
                    packet(number)

        return carry

    lax.fori_loop(0, PARTS, forward, 0)

    passing = neighbour(1)[1]
    behind = jnp.logical_and(passing, place_in_row == 0)

    def pass_on(index, carry):
        at = quarter(index)
        drain(qg.at[1, :, at, :], far_recv.at[1, index])
        remote(
            qg.at[1, :, at, :], qg.at[3, :, at, :],
            far_send.at[2, index], far_recv.at[3, index], seq=neighbour(0)[0],
        ).start()
        return carry

    drain(delta_in, delta_recv)
    for at in range(lanes):
        rows_of[OWN, 1:2, at * HD : (at + 1) * HD] = delta_in[2 * at] + delta_in[2 * at + 1]
    for slot in range(SLOTS):
        other, inside = neighbour(slot)

        @pl.when(standing(slot)[3])
        def _(slot=slot, other=other):
            pl.semaphore_wait(ready.at[slot], 1)
            if slot != 2:
                for index in range(PARTS):
                    forward_piece(slot, index, other)

        @pl.when(inside)
        def _(slot=slot, other=other):
            there = slot if slot < 2 else 5 - slot
            remote(rows_of.at[OWN], rows_of.at[there], rows_send.at[slot], rows_recv.at[there], seq=other).start()

    @pl.when(jnp.logical_and(passing, jnp.logical_not(behind)))
    def _():
        lax.fori_loop(0, PARTS, pass_on, 0)

    def arrive(index):
        at = quarter(index)
        drain(kv.at[:, at, :], kv_recv.at[index])

        @pl.when(index == 0)
        def _():
            for number in range(AFTER[-1][1][-1] + 1, 2 * PARTS):
                packet(number)

        key_t[index] = kv[0, at, :].T

    def item(index, slot):
        at = quarter(index)
        query_rows = qg[slot, 0]
        grad_rows = qg[slot, 1]
        scores = dot(kv[0, at, :], query_rows, NT)
        probs = jnp.exp2(scores * (SCALE * LOG2E) - rows_of[slot, 0:1, :])
        grad_prob = dot(kv[1, at, :], grad_rows, NT)
        probs_low = probs.astype(jnp.bfloat16)
        grad_score = (probs * (grad_prob - rows_of[slot, 1:2, :])).astype(jnp.bfloat16)
        acc_value[at, :] += dot(probs_low, grad_rows, NN)
        acc_key[at, :] += dot(grad_score, query_rows, NN)
        acc_query[slot] += dot(key_t[index], grad_score, NN)

    def far_item(index, slot):
        other, inside = neighbour(slot)

        @pl.when(inside)
        def _():
            @pl.when(index == 0)
            def _():
                drain(rows_of.at[slot], rows_recv.at[slot])
                listed = band[here - other + R, other] == 1
                rows_of[slot, 0:1, :] = jnp.where(listed, rows_of[slot, 0:1, :], UNLISTED)

                @pl.when(jnp.logical_not(jnp.logical_and(slot == 1, passing)))
                def _():
                    for piece in range(PARTS):
                        drain(qg.at[slot, :, pl.ds(piece * chunk, chunk), :], far_recv.at[slot, piece])

            item(index, slot)

            @pl.when(index == PARTS - 1)
            def _():
                there = far_slot(slot)
                for piece in range(PARTS):
                    lanes_of = slice(piece * chunk, (piece + 1) * chunk)
                    term_out[slot, piece] = acc_query[slot, :, lanes_of].astype(jnp.bfloat16)
                    remote(
                        term_out.at[slot, piece], term_in.at[there, piece],
                        term_send.at[slot], term_recv.at[there, piece], seq=other,
                    ).start()

    def send_rows(src, dst, which, place):
        to = sender(place)
        remote(src.at[part(place), :], dst.at[:, cols(head)], res_send.at[which], res_recv.at[which], head=to).start()

    def send_own(src, dst, which):
        pltpu.make_async_copy(src.at[part(0), :], dst.at[:, cols(head)], res_recv.at[which]).start()

    def finish(index):
        at = quarter(index)
        res_kv[0, at, :] = acc_key[at, :].astype(jnp.bfloat16)
        res_kv[1, at, :] = (acc_value[at, :] * (1.0 / SCALE)).astype(jnp.bfloat16)

        def step(place, carry):
            @pl.when(place > 0)
            def _():
                send_rows(res_kv.at[0], out_key, 1, place)
                send_rows(res_kv.at[1], out_value, 2, place)

            return carry

        lax.fori_loop(index * per, index * per + per, step, 0)

    def first_pass(index, carry):
        arrive(index)
        item(index, OWN)

        def step(turn, carry):
            far_item(index, ordered(turn))
            return carry

        return lax.fori_loop(0, NEAR, step, carry)

    def second_pass(index, carry):
        def step(turn, carry):
            far_item(index, ordered(turn))
            return carry

        lax.fori_loop(NEAR, SLOTS, step, 0)
        finish(index)
        return carry

    lax.fori_loop(0, PARTS, first_pass, 0)

    @pl.when(behind)
    def _():
        lax.fori_loop(0, PARTS, pass_on, 0)

    lax.fori_loop(0, PARTS, second_pass, 0)
    send_own(res_kv.at[0], out_key, 1)
    send_own(res_kv.at[1], out_value, 2)

    def query_part(index, carry):
        at = quarter(index)
        acc_part[...] = acc_query[OWN, :, at]
        for slot in range(SLOTS):

            @pl.when(neighbour(slot)[1])
            def _(slot=slot):
                drain(term_in.at[slot, index], term_recv.at[slot, index])
                acc_part[...] += term_in[slot, index].astype(jnp.float32)

        res_query[at, :] = acc_part[...].T.astype(jnp.bfloat16)

        def step(place, carry):
            @pl.when(place > 0)
            def _():
                send_rows(res_query, out_query, 0, place)

            return carry

        lax.fori_loop(index * per, index * per + per, step, 0)
        return carry

    lax.fori_loop(0, PARTS, query_part, 0)
    send_own(res_query, out_query, 0)

    sent = pl.ds(0, (nhead - 1) * rows)
    drain(qg.at[OWN, :, sent, :], qg_send)
    drain(kv.at[:, sent, :], kv_send)
    drain(delta_in.at[pl.ds(0, nhead - 1)], delta_send)
    for slot in range(SLOTS):
        inside = neighbour(slot)[1]

        @pl.when(passing if slot == 2 else inside)
        def _(slot=slot):
            for piece in range(PARTS):
                drain(qg.at[OWN, :, pl.ds(piece * chunk, chunk), :], far_send.at[slot, piece])

        @pl.when(inside)
        def _(slot=slot):
            drain(rows_of.at[OWN], rows_send.at[slot])
            drain(term_out.at[slot], term_send.at[slot])

    for which in range(3):
        drain(res_query.at[sent, :], res_send.at[which])
    drain(out_key, res_recv.at[1])
    drain(out_value, res_recv.at[2])
    drain(out_query, res_recv.at[0])


def per_device(query, key, value, attn_out, grad_out, lse, band):
    nseq, nhead = lax.axis_size("seq"), lax.axis_size("head")
    rows, width = query.shape
    block = rows * nhead
    low, full = jnp.bfloat16, jnp.float32
    vmem = pl.BlockSpec(memory_space=pltpu.VMEM)
    hbm = pl.BlockSpec(memory_space=pltpu.HBM)
    result = jax.ShapeDtypeStruct((rows, width), low)
    dma = pltpu.SemaphoreType.DMA

    def body(*refs):
        kernel(nseq, nhead, *refs)

    return pl.pallas_call(
        body,
        out_shape=(result,) * 3,
        in_specs=[hbm] * 6 + [pl.BlockSpec(memory_space=pltpu.SMEM)],
        out_specs=[vmem] * 3,
        scratch_shapes=[pltpu.VMEM((rows, width), low)] * 5
        + [
            pltpu.VMEM((1, block), full),
            pltpu.VMEM((block // HD, HD), full),
            pltpu.VMEM((HD, HD), full),
            pltpu.VMEM((SLOTS + 1, 2, block, HD), low),
            pltpu.VMEM((2, block, HD), low),
            pltpu.VMEM((SLOTS + 1, 2, block), full),
            pltpu.VMEM((nhead, 1, HD), full),
            pltpu.VMEM((nhead, 1, HD), full),
            pltpu.VMEM((PARTS, HD, block // PARTS), low),
            pltpu.VMEM((SLOTS + 1, HD, block), full),
            pltpu.VMEM((HD, block // PARTS), full),
            pltpu.VMEM((block, HD), full),
            pltpu.VMEM((block, HD), full),
            pltpu.VMEM((SLOTS, PARTS, HD, block // PARTS), low),
            pltpu.VMEM((SLOTS, PARTS, HD, block // PARTS), low),
            pltpu.VMEM((block, HD), low),
            pltpu.VMEM((2, block, HD), low),
            dma((6,)),
            dma, dma((PARTS,)), dma, dma((PARTS,)), dma, dma,
            dma((SLOTS, PARTS)), dma((SLOTS, PARTS)),
            dma((SLOTS,)), dma((SLOTS,)),
            dma((SLOTS,)), dma((SLOTS, PARTS)),
            dma((3,)), dma((3,)),
            pltpu.SemaphoreType.REGULAR((SLOTS,)),
        ],
        compiler_params=pltpu.CompilerParams(
            collective_id=0, has_side_effects=True, vmem_limit_bytes=62 * 2**20
        ),
        cost_estimate=pl.CostEstimate(
            flops=25 * 2 * block * block * HD, bytes_accessed=8 * rows * width * 2,
            transcendentals=5 * block * block,
        ),
        name="attention_grads",
    )(query, key, value, attn_out, grad_out, lse, band.T)


def solution(mesh):
    rows = P(("seq", "head"), None)
    return jax.shard_map(
        per_device, mesh=mesh, in_specs=(rows,) * 5 + (P("head", "seq"), P()),
        out_specs=(rows,) * 3, check_vma=False,
    )
```

```python
import math

import jax
import jax.numpy as jnp
from jax import lax
from jax.experimental import pallas as pl
from jax.experimental.pallas import tpu as pltpu
from jax.sharding import PartitionSpec as P

R = 2
HD = 128
SLOTS = 2 * R
OWN = SLOTS
PARTS = 4
FIRST = 4
AFTER = ((1, (4,)), (2, (5,)), (3, (6,)))
LOG2E = 1.4426950408889634
SCALE = 1.0 / math.sqrt(HD)
UNLISTED = 1e30
MESH = pl.DeviceIdType.MESH
NT = (((1,), (1,)), ((), ()))
NN = (((1,), (0,)), ((), ()))


def dot(a, b, dims):
    return lax.dot_general(a, b, dims, preferred_element_type=jnp.float32)


def slot_step(slot, sign):
    return sign * (1 + slot // 2) * (1 - 2 * ((slot * (3 - slot)) // 2))


def far_slot(slot):
    return jnp.where(slot < 2, slot, 5 - slot)


def kernel(
    nseq,
    nhead,
    query_hbm,
    key_hbm,
    value_hbm,
    attn_out_hbm,
    grad_out_hbm,
    lse_hbm,
    band,
    out_query,
    out_key,
    out_value,
    query,
    key,
    value,
    attn_out,
    grad_out,
    lse,
    lse_rows,
    across,
    qg,
    kv,
    rows_of,
    delta_out,
    delta_in,
    key_t,
    acc_query,
    acc_part,
    acc_key,
    acc_value,
    term_out,
    term_in,
    res_query,
    res_kv,
    load_sem,
    qg_send,
    qg_recv,
    kv_send,
    kv_recv,
    delta_send,
    delta_recv,
    far_send,
    far_recv,
    rows_send,
    rows_recv,
    term_send,
    term_recv,
    res_send,
    res_recv,
    ready,
):
    here = lax.axis_index("seq")
    head = lax.axis_index("head")
    sign = 1 - 2 * lax.rem(here, 2)
    row = nseq // 2 if nseq >= 8 * R else nseq
    place_in_row = lax.rem(here, row)
    at_end = jnp.logical_or(place_in_row == 0, place_in_row == row - 1)
    beside_end = jnp.logical_or(place_in_row == 1, place_in_row == row - 2)
    rows = query.shape[0]
    block = rows * nhead
    chunk = block // PARTS
    per = nhead // PARTS
    ny = nhead // 2

    def cols(which):
        return pl.ds(pl.multiple_of(which * HD, HD), HD)

    def part(which):
        return pl.ds(pl.multiple_of(which * rows, rows), rows)

    def quarter(which):
        return pl.ds(pl.multiple_of(which * chunk, chunk), chunk)

    def offset(place):
        if ny != 8:
            return place // 2, place % 2
        group, which = place // 4, place % 4
        reach = jnp.where(group == 3, 2, 1 + 2 * (which // 2))
        along_y = jnp.where(which % 2 == 1, ny - reach, reach)
        along_y = jnp.where(group == 0, 4 * (which // 2), along_y)
        along_x = jnp.where(group == 0, which % 2, jnp.where(group == 3, which // 2, group - 1))
        return along_y, along_x

    def sender(place):
        along_y, along_x = offset(place)
        return 2 * lax.rem(head // 2 + ny - along_y, ny) + lax.rem(head + along_x, 2)

    def receiver(place):
        along_y, along_x = offset(place)
        return 2 * lax.rem(head // 2 + along_y, ny) + lax.rem(head + along_x, 2)

    def after(step):
        return lax.rem(head + step, nhead)

    def neighbour(slot):
        other = here + slot_step(slot, sign)
        return other, jnp.logical_and(other >= 0, other < nseq)

    def standing(slot):
        other, inside = neighbour(slot)
        ahead = lax.rem(other + nseq, row) - place_in_row
        later = jnp.logical_and(inside, ahead > 0)
        earlier = jnp.logical_and(inside, ahead < 0)
        return other, later, earlier, jnp.logical_and(inside, ahead > R)

    def ordered(turn):
        early_last = jnp.where(turn == 1, 3, jnp.where(turn > 1, turn - 1, 0))
        late_first = jnp.where(turn > 1, 5 - turn, turn)
        slot = jnp.where(place_in_row == 0, early_last, turn)
        return jnp.where(place_in_row >= row - 2, late_first, slot)

    near = jnp.where(at_end, 1, 2)
    whole = jnp.where(jnp.logical_or(at_end, beside_end), 1, 0)

    def remote(src, dst, send, recv, **where):
        return pltpu.make_async_remote_copy(
            src_ref=src, dst_ref=dst, send_sem=send, recv_sem=recv,
            device_id=where, device_id_type=MESH,
        )

    def drain(ref, sem):
        pltpu.make_async_copy(ref, ref, sem).wait()

    loads = [
        pltpu.make_async_copy(src, dst, load_sem.at[at])
        for at, (src, dst) in enumerate(
            (
                (query_hbm, query),
                (grad_out_hbm, grad_out),
                (attn_out_hbm, attn_out),
                (key_hbm, key),
                (value_hbm, value),
                (lse_hbm, lse),
            )
        )
    ]
    for load in loads:
        load.start()

    barrier = pltpu.get_barrier_semaphore()

    def greet(step, carry):
        pl.semaphore_signal(barrier, inc=1, device_id={"head": after(step)}, device_id_type=MESH)
        return carry

    lax.fori_loop(1, nhead, greet, 0)
    count = nhead - 1
    for slot in range(SLOTS):
        other, later, earlier, _ = standing(slot)
        count = count + jnp.where(earlier, 1, 0)

        @pl.when(later)
        def _(other=other):
            pl.semaphore_signal(barrier, inc=1, device_id={"seq": other}, device_id_type=MESH)

    pl.semaphore_wait(barrier, count)
    for slot in range(SLOTS):
        other, _, earlier, _ = standing(slot)

        @pl.when(earlier)
        def _(slot=slot, other=other):
            there = slot if slot < 2 else 5 - slot
            pl.semaphore_signal(ready.at[there], inc=1, device_id={"seq": other}, device_id_type=MESH)

    def exchange(first, second, dst, send, recv, index):
        def step(place, carry):
            to = receiver(place)

            @pl.when(place > 0)
            def _():
                remote(first.at[:, cols(to)], dst.at[0, part(place), :], send, recv.at[index], head=to).start()
                remote(second.at[:, cols(to)], dst.at[1, part(place), :], send, recv.at[index], head=to).start()

            return carry

        lax.fori_loop(index * per, index * per + per, step, 0)

    def packet(number):
        if number < PARTS:
            exchange(query, grad_out, qg.at[OWN], qg_send, qg_recv, number)
        else:
            exchange(key, value, kv, kv_send, kv_recv, number - PARTS)

    for load in loads[:2] + loads[3:5]:
        load.wait()
    for number in range(FIRST):
        packet(number)
    for at, (first, second) in enumerate(((query, grad_out), (key, value))):
        dst, recv = ((qg.at[OWN], qg_recv), (kv, kv_recv))[at]
        pltpu.make_async_copy(first.at[:, cols(head)], dst.at[0, part(0), :], recv.at[0]).start()
        pltpu.make_async_copy(second.at[:, cols(head)], dst.at[1, part(0), :], recv.at[0]).start()

    loads[2].wait()
    lane = lax.broadcasted_iota(jnp.int32, (rows, HD), 1)
    sums = jnp.zeros((rows, HD), jnp.float32)
    for which in range(nhead):
        at = slice(which * HD, (which + 1) * HD)
        product = grad_out[:, at].astype(jnp.float32) * attn_out[:, at].astype(jnp.float32)
        sums = jnp.where(lane == which, jnp.sum(product, axis=1, keepdims=True), sums)
    across[...] = jnp.concatenate([sums, sums], axis=0).T
    low_half = lax.broadcasted_iota(jnp.int32, (1, HD), 1) < rows
    for place in range(nhead):
        to = receiver(place)
        mine = low_half if place % 2 == 0 else jnp.logical_not(low_half)
        delta_out[place] = jnp.where(mine, across[pl.ds(to, 1), :], 0.0)
        if place:
            remote(delta_out.at[place], delta_in.at[place], delta_send, delta_recv, head=to).start()
        else:
            pltpu.make_async_copy(delta_out.at[0], delta_in.at[0], delta_recv).start()

    loads[5].wait()
    lanes = block // HD
    for at in range(lanes):
        lse_rows[at : at + 1, :] = lse[:, at * HD : (at + 1) * HD]

    def lse_half(place):
        source = sender(place)
        one = lse_rows[pl.ds(source // 2, 1), :]
        other = jnp.concatenate([one[:, rows:], one[:, :rows]], axis=1)
        return jnp.where(lax.rem(source, 2) == place % 2, one, other)

    for at in range(lanes):
        turned = jnp.where(low_half, lse_half(2 * at), lse_half(2 * at + 1))
        rows_of[OWN, 0:1, at * HD : (at + 1) * HD] = turned * LOG2E + math.log2(1.0 / SCALE)
    acc_query[...] = jnp.zeros_like(acc_query)
    acc_key[...] = jnp.zeros_like(acc_key)
    acc_value[...] = jnp.zeros_like(acc_value)

    def forward_piece(slot, index, other):
        there = slot if slot < 2 else 5 - slot
        at = quarter(index)
        remote(
            qg.at[OWN, :, at, :], qg.at[there, :, at, :],
            far_send.at[slot, index], far_recv.at[there, index], seq=other,
        ).start()

    def forward(index, carry):
        drain(qg.at[OWN, :, quarter(index), :], qg_recv.at[index])
        for slot in range(SLOTS):
            other, later, earlier, late = standing(slot)
            prompt = jnp.logical_and(later, jnp.logical_not(late))
            @pl.when(prompt)
            def _(slot=slot, other=other):
                @pl.when(index == 0)
                def _():
                    pl.semaphore_wait(ready.at[slot], 1)

                if slot != 2:
                    forward_piece(slot, index, other)

            @pl.when(jnp.logical_and(earlier, slot != 2))
            def _(slot=slot, other=other):
                forward_piece(slot, index, other)

        for moment, numbers in AFTER:

            @pl.when(index == moment)
            def _(numbers=numbers):
                for number in numbers:
                    packet(number)

        return carry

    lax.fori_loop(0, PARTS, forward, 0)

    passing = neighbour(1)[1]

    def pass_on(index, carry):
        at = quarter(index)
        drain(qg.at[1, :, at, :], far_recv.at[1, index])
        remote(
            qg.at[1, :, at, :], qg.at[3, :, at, :],
            far_send.at[2, index], far_recv.at[3, index], seq=neighbour(0)[0],
        ).start()
        return carry

    drain(delta_in, delta_recv)
    for at in range(lanes):
        rows_of[OWN, 1:2, at * HD : (at + 1) * HD] = delta_in[2 * at] + delta_in[2 * at + 1]
    for slot in range(SLOTS):
        other, inside = neighbour(slot)

        @pl.when(standing(slot)[3])
        def _(slot=slot, other=other):
            pl.semaphore_wait(ready.at[slot], 1)
            if slot != 2:
                for index in range(PARTS):
                    forward_piece(slot, index, other)

        @pl.when(inside)
        def _(slot=slot, other=other):
            there = slot if slot < 2 else 5 - slot
            remote(rows_of.at[OWN], rows_of.at[there], rows_send.at[slot], rows_recv.at[there], seq=other).start()

    def arrive(index):
        at = quarter(index)
        drain(kv.at[:, at, :], kv_recv.at[index])

        @pl.when(index == 0)
        def _():
            for number in range(AFTER[-1][1][-1] + 1, 2 * PARTS):
                packet(number)

        key_t[index] = kv[0, at, :].T

    def item(index, slot):
        at = quarter(index)
        query_rows = qg[slot, 0]
        grad_rows = qg[slot, 1]
        scores = dot(kv[0, at, :], query_rows, NT)
        probs = jnp.exp2(scores * (SCALE * LOG2E) - rows_of[slot, 0:1, :])
        grad_prob = dot(kv[1, at, :], grad_rows, NT)
        probs_low = probs.astype(jnp.bfloat16)
        grad_score = (probs * (grad_prob - rows_of[slot, 1:2, :])).astype(jnp.bfloat16)
        acc_value[at, :] += dot(probs_low, grad_rows, NN)
        acc_key[at, :] += dot(grad_score, query_rows, NN)
        acc_query[slot] += dot(key_t[index], grad_score, NN)

    def far_item(index, slot):
        other, inside = neighbour(slot)

        @pl.when(inside)
        def _():
            @pl.when(index == 0)
            def _():
                drain(rows_of.at[slot], rows_recv.at[slot])
                listed = band[here - other + R, other] == 1
                rows_of[slot, 0:1, :] = jnp.where(listed, rows_of[slot, 0:1, :], UNLISTED)

                @pl.when(slot == 1)
                def _():
                    lax.fori_loop(0, PARTS, pass_on, 0)

                @pl.when(slot != 1)
                def _():
                    for piece in range(PARTS):
                        drain(qg.at[slot, :, pl.ds(piece * chunk, chunk), :], far_recv.at[slot, piece])

            item(index, slot)

            @pl.when(index == PARTS - 1)
            def _():
                there = far_slot(slot)
                for piece in range(PARTS):
                    lanes_of = slice(piece * chunk, (piece + 1) * chunk)
                    term_out[slot, piece] = acc_query[slot, :, lanes_of].astype(jnp.bfloat16)
                    remote(
                        term_out.at[slot, piece], term_in.at[there, piece],
                        term_send.at[slot], term_recv.at[there, piece], seq=other,
                    ).start()

    def send_rows(src, dst, which, place):
        to = sender(place)
        remote(src.at[part(place), :], dst.at[:, cols(head)], res_send.at[which], res_recv.at[which], head=to).start()

    def send_own(src, dst, which):
        pltpu.make_async_copy(src.at[part(0), :], dst.at[:, cols(head)], res_recv.at[which]).start()

    def finish(index):
        at = quarter(index)
        res_kv[0, at, :] = acc_key[at, :].astype(jnp.bfloat16)
        res_kv[1, at, :] = (acc_value[at, :] * (1.0 / SCALE)).astype(jnp.bfloat16)

        def step(place, carry):
            @pl.when(place > 0)
            def _():
                send_rows(res_kv.at[0], out_key, 1, place)
                send_rows(res_kv.at[1], out_value, 2, place)

            return carry

        lax.fori_loop(index * per, index * per + per, step, 0)

    def first_pass(index, carry):
        arrive(index)
        item(index, OWN)

        def step(turn, carry):
            far_item(index, ordered(turn))
            return carry

        return lax.fori_loop(0, near, step, carry)

    def whole_pass(turn, carry):
        def step(index, carry):
            far_item(index, ordered(turn))
            return carry

        return lax.fori_loop(0, PARTS, step, carry)

    def second_pass(index, carry):
        def step(turn, carry):
            far_item(index, ordered(turn))
            return carry

        lax.fori_loop(near + whole, SLOTS, step, 0)
        finish(index)
        return carry

    lax.fori_loop(0, PARTS, first_pass, 0)
    lax.fori_loop(near, near + whole, whole_pass, 0)
    lax.fori_loop(0, PARTS, second_pass, 0)
    send_own(res_kv.at[0], out_key, 1)
    send_own(res_kv.at[1], out_value, 2)

    def query_part(index, carry):
        at = quarter(index)
        acc_part[...] = acc_query[OWN, :, at]
        for slot in range(SLOTS):

            @pl.when(neighbour(slot)[1])
            def _(slot=slot):
                drain(term_in.at[slot, index], term_recv.at[slot, index])
                acc_part[...] += term_in[slot, index].astype(jnp.float32)

        res_query[at, :] = acc_part[...].T.astype(jnp.bfloat16)

        def step(place, carry):
            @pl.when(place > 0)
            def _():
                send_rows(res_query, out_query, 0, place)

            return carry

        lax.fori_loop(index * per, index * per + per, step, 0)
        return carry

    lax.fori_loop(0, PARTS, query_part, 0)
    send_own(res_query, out_query, 0)

    sent = pl.ds(0, (nhead - 1) * rows)
    drain(qg.at[OWN, :, sent, :], qg_send)
    drain(kv.at[:, sent, :], kv_send)
    drain(delta_in.at[pl.ds(0, nhead - 1)], delta_send)
    for slot in range(SLOTS):
        inside = neighbour(slot)[1]

        @pl.when(passing if slot == 2 else inside)
        def _(slot=slot):
            for piece in range(PARTS):
                drain(qg.at[OWN, :, pl.ds(piece * chunk, chunk), :], far_send.at[slot, piece])

        @pl.when(inside)
        def _(slot=slot):
            drain(rows_of.at[OWN], rows_send.at[slot])
            drain(term_out.at[slot], term_send.at[slot])

    for which in range(3):
        drain(res_query.at[sent, :], res_send.at[which])
    drain(out_key, res_recv.at[1])
    drain(out_value, res_recv.at[2])
    drain(out_query, res_recv.at[0])


def per_device(query, key, value, attn_out, grad_out, lse, band):
    nseq, nhead = lax.axis_size("seq"), lax.axis_size("head")
    rows, width = query.shape
    block = rows * nhead
    low, full = jnp.bfloat16, jnp.float32
    vmem = pl.BlockSpec(memory_space=pltpu.VMEM)
    hbm = pl.BlockSpec(memory_space=pltpu.HBM)
    result = jax.ShapeDtypeStruct((rows, width), low)
    dma = pltpu.SemaphoreType.DMA

    def body(*refs):
        kernel(nseq, nhead, *refs)

    return pl.pallas_call(
        body,
        out_shape=(result,) * 3,
        in_specs=[hbm] * 6 + [pl.BlockSpec(memory_space=pltpu.SMEM)],
        out_specs=[hbm] * 3,
        scratch_shapes=[pltpu.VMEM((rows, width), low)] * 5
        + [
            pltpu.VMEM((1, block), full),
            pltpu.VMEM((block // HD, HD), full),
            pltpu.VMEM((HD, HD), full),
            pltpu.VMEM((SLOTS + 1, 2, block, HD), low),
            pltpu.VMEM((2, block, HD), low),
            pltpu.VMEM((SLOTS + 1, 2, block), full),
            pltpu.VMEM((nhead, 1, HD), full),
            pltpu.VMEM((nhead, 1, HD), full),
            pltpu.VMEM((PARTS, HD, block // PARTS), low),
            pltpu.VMEM((SLOTS + 1, HD, block), full),
            pltpu.VMEM((HD, block // PARTS), full),
            pltpu.VMEM((block, HD), full),
            pltpu.VMEM((block, HD), full),
            pltpu.VMEM((SLOTS, PARTS, HD, block // PARTS), low),
            pltpu.VMEM((SLOTS, PARTS, HD, block // PARTS), low),
            pltpu.VMEM((block, HD), low),
            pltpu.VMEM((2, block, HD), low),
            dma((6,)),
            dma, dma((PARTS,)), dma, dma((PARTS,)), dma, dma,
            dma((SLOTS, PARTS)), dma((SLOTS, PARTS)),
            dma((SLOTS,)), dma((SLOTS,)),
            dma((SLOTS,)), dma((SLOTS, PARTS)),
            dma((3,)), dma((3,)),
            pltpu.SemaphoreType.REGULAR((SLOTS,)),
        ],
        compiler_params=pltpu.CompilerParams(
            collective_id=0, has_side_effects=True, vmem_limit_bytes=62 * 2**20
        ),
        cost_estimate=pl.CostEstimate(
            flops=25 * 2 * block * block * HD, bytes_accessed=8 * rows * width * 2,
            transcendentals=5 * block * block,
        ),
        name="attention_grads",
    )(query, key, value, attn_out, grad_out, lse, band.T)


def solution(mesh):
    rows = P(("seq", "head"), None)
    return jax.shard_map(
        per_device, mesh=mesh, in_specs=(rows,) * 5 + (P("head", "seq"), P()),
        out_specs=(rows,) * 3, check_vma=False,
    )
```

```python
import math

import jax
import jax.numpy as jnp
from jax import lax
from jax.experimental import pallas as pl
from jax.experimental.pallas import tpu as pltpu
from jax.sharding import PartitionSpec as P

R = 2
HD = 128
SLOTS = 2 * R
OWN = SLOTS
PARTS = 4
FIRST = 4
AFTER = ((1, (4,)), (2, (5,)), (3, (6,)))
LOG2E = 1.4426950408889634
SCALE = 1.0 / math.sqrt(HD)
UNLISTED = 1e30
MESH = pl.DeviceIdType.MESH
NT = (((1,), (1,)), ((), ()))
NN = (((1,), (0,)), ((), ()))


def dot(a, b, dims):
    return lax.dot_general(a, b, dims, preferred_element_type=jnp.float32)


def slot_step(slot, sign):
    return sign * (1 + slot // 2) * (1 - 2 * ((slot * (3 - slot)) // 2))


def far_slot(slot):
    return jnp.where(slot < 2, slot, 5 - slot)


def kernel(
    nseq,
    nhead,
    query_hbm,
    key_hbm,
    value_hbm,
    attn_out_hbm,
    grad_out_hbm,
    lse_hbm,
    band,
    out_query,
    out_key,
    out_value,
    query,
    key,
    value,
    attn_out,
    grad_out,
    lse,
    lse_rows,
    across,
    qg,
    kv,
    rows_of,
    delta_out,
    delta_in,
    key_t,
    acc_query,
    acc_part,
    acc_key,
    acc_value,
    term_out,
    term_in,
    res_query,
    res_kv,
    load_sem,
    qg_send,
    qg_recv,
    kv_send,
    kv_recv,
    delta_send,
    delta_recv,
    far_send,
    far_recv,
    rows_send,
    rows_recv,
    term_send,
    term_recv,
    res_send,
    res_recv,
    ready,
):
    here = lax.axis_index("seq")
    head = lax.axis_index("head")
    sign = 1 - 2 * lax.rem(here, 2)
    row = nseq // 2 if nseq >= 8 * R else nseq
    place_in_row = lax.rem(here, row)
    at_end = jnp.logical_or(place_in_row == 0, place_in_row == row - 1)
    beside_end = jnp.logical_or(place_in_row == 1, place_in_row == row - 2)
    rows = query.shape[0]
    block = rows * nhead
    chunk = block // PARTS
    per = nhead // PARTS
    ny = nhead // 2

    def cols(which):
        return pl.ds(pl.multiple_of(which * HD, HD), HD)

    def part(which):
        return pl.ds(pl.multiple_of(which * rows, rows), rows)

    def quarter(which):
        return pl.ds(pl.multiple_of(which * chunk, chunk), chunk)

    def offset(place):
        if ny != 8:
            return place // 2, place % 2
        group, which = place // 4, place % 4
        reach = jnp.where(group == 3, 2, 1 + 2 * (which // 2))
        along_y = jnp.where(which % 2 == 1, ny - reach, reach)
        along_y = jnp.where(group == 0, 4 * (which // 2), along_y)
        along_x = jnp.where(group == 0, which % 2, jnp.where(group == 3, which // 2, group - 1))
        return along_y, along_x

    def sender(place):
        along_y, along_x = offset(place)
        return 2 * lax.rem(head // 2 + ny - along_y, ny) + lax.rem(head + along_x, 2)

    def receiver(place):
        along_y, along_x = offset(place)
        return 2 * lax.rem(head // 2 + along_y, ny) + lax.rem(head + along_x, 2)

    def after(step):
        return lax.rem(head + step, nhead)

    def neighbour(slot):
        other = here + slot_step(slot, sign)
        return other, jnp.logical_and(other >= 0, other < nseq)

    def standing(slot):
        other, inside = neighbour(slot)
        ahead = lax.rem(other + nseq, row) - place_in_row
        later = jnp.logical_and(inside, ahead > 0)
        earlier = jnp.logical_and(inside, ahead < 0)
        return other, later, earlier, jnp.logical_and(inside, ahead > R)

    def ordered(turn):
        early_last = jnp.where(turn == 1, 3, jnp.where(turn > 1, turn - 1, 0))
        late_first = jnp.where(turn > 1, 5 - turn, turn)
        slot = jnp.where(place_in_row == 0, early_last, turn)
        return jnp.where(place_in_row >= row - 2, late_first, slot)

    near = jnp.where(at_end, 1, 2)
    whole = jnp.where(jnp.logical_or(at_end, beside_end), 1, 0)

    def remote(src, dst, send, recv, **where):
        return pltpu.make_async_remote_copy(
            src_ref=src, dst_ref=dst, send_sem=send, recv_sem=recv,
            device_id=where, device_id_type=MESH,
        )

    def drain(ref, sem):
        pltpu.make_async_copy(ref, ref, sem).wait()

    loads = [
        pltpu.make_async_copy(src, dst, load_sem.at[at])
        for at, (src, dst) in enumerate(
            (
                (query_hbm, query),
                (grad_out_hbm, grad_out),
                (attn_out_hbm, attn_out),
                (key_hbm, key),
                (value_hbm, value),
                (lse_hbm, lse),
            )
        )
    ]
    for load in loads:
        load.start()

    barrier = pltpu.get_barrier_semaphore()

    def greet(step, carry):
        pl.semaphore_signal(barrier, inc=1, device_id={"head": after(step)}, device_id_type=MESH)
        return carry

    lax.fori_loop(1, nhead, greet, 0)
    count = nhead - 1
    for slot in range(SLOTS):
        other, later, earlier, _ = standing(slot)
        count = count + jnp.where(earlier, 1, 0)

        @pl.when(later)
        def _(other=other):
            pl.semaphore_signal(barrier, inc=1, device_id={"seq": other}, device_id_type=MESH)

    pl.semaphore_wait(barrier, count)
    for slot in range(SLOTS):
        other, _, earlier, _ = standing(slot)

        @pl.when(earlier)
        def _(slot=slot, other=other):
            there = slot if slot < 2 else 5 - slot
            pl.semaphore_signal(ready.at[there], inc=1, device_id={"seq": other}, device_id_type=MESH)

    def exchange(first, second, dst, send, recv, index):
        def step(place, carry):
            to = receiver(place)

            @pl.when(place > 0)
            def _():
                remote(first.at[:, cols(to)], dst.at[0, part(place), :], send, recv.at[index], head=to).start()
                remote(second.at[:, cols(to)], dst.at[1, part(place), :], send, recv.at[index], head=to).start()

            return carry

        lax.fori_loop(index * per, index * per + per, step, 0)

    def packet(number):
        if number < PARTS:
            exchange(query, grad_out, qg.at[OWN], qg_send, qg_recv, number)
        else:
            exchange(key, value, kv, kv_send, kv_recv, number - PARTS)

    for load in loads[:2] + loads[3:5]:
        load.wait()
    for number in range(FIRST):
        packet(number)
    for at, (first, second) in enumerate(((query, grad_out), (key, value))):
        dst, recv = ((qg.at[OWN], qg_recv), (kv, kv_recv))[at]
        pltpu.make_async_copy(first.at[:, cols(head)], dst.at[0, part(0), :], recv.at[0]).start()
        pltpu.make_async_copy(second.at[:, cols(head)], dst.at[1, part(0), :], recv.at[0]).start()

    loads[2].wait()
    lane = lax.broadcasted_iota(jnp.int32, (rows, HD), 1)
    sums = jnp.zeros((rows, HD), jnp.float32)
    for which in range(nhead):
        at = slice(which * HD, (which + 1) * HD)
        product = grad_out[:, at].astype(jnp.float32) * attn_out[:, at].astype(jnp.float32)
        sums = jnp.where(lane == which, jnp.sum(product, axis=1, keepdims=True), sums)
    across[...] = jnp.concatenate([sums, sums], axis=0).T
    low_half = lax.broadcasted_iota(jnp.int32, (1, HD), 1) < rows
    for place in range(nhead):
        to = receiver(place)
        mine = low_half if place % 2 == 0 else jnp.logical_not(low_half)
        delta_out[place] = jnp.where(mine, across[pl.ds(to, 1), :], 0.0)
        if place:
            remote(delta_out.at[place], delta_in.at[place], delta_send, delta_recv, head=to).start()
        else:
            pltpu.make_async_copy(delta_out.at[0], delta_in.at[0], delta_recv).start()

    loads[5].wait()
    lanes = block // HD
    for at in range(lanes):
        lse_rows[at : at + 1, :] = lse[:, at * HD : (at + 1) * HD]

    def lse_half(place):
        source = sender(place)
        one = lse_rows[pl.ds(source // 2, 1), :]
        other = jnp.concatenate([one[:, rows:], one[:, :rows]], axis=1)
        return jnp.where(lax.rem(source, 2) == place % 2, one, other)

    for at in range(lanes):
        turned = jnp.where(low_half, lse_half(2 * at), lse_half(2 * at + 1))
        rows_of[OWN, 0:1, at * HD : (at + 1) * HD] = turned * LOG2E + math.log2(1.0 / SCALE)
    acc_query[...] = jnp.zeros_like(acc_query)
    acc_key[...] = jnp.zeros_like(acc_key)
    acc_value[...] = jnp.zeros_like(acc_value)

    def forward_piece(slot, index, other):
        there = slot if slot < 2 else 5 - slot
        at = quarter(index)
        remote(
            qg.at[OWN, :, at, :], qg.at[there, :, at, :],
            far_send.at[slot, index], far_recv.at[there, index], seq=other,
        ).start()

    def forward(index, carry):
        drain(qg.at[OWN, :, quarter(index), :], qg_recv.at[index])
        for slot in range(SLOTS):
            other, later, earlier, late = standing(slot)
            prompt = jnp.logical_and(later, jnp.logical_not(late))
            @pl.when(prompt)
            def _(slot=slot, other=other):
                @pl.when(index == 0)
                def _():
                    pl.semaphore_wait(ready.at[slot], 1)

                if slot != 2:
                    forward_piece(slot, index, other)

            @pl.when(jnp.logical_and(earlier, slot != 2))
            def _(slot=slot, other=other):
                forward_piece(slot, index, other)

        for moment, numbers in AFTER:

            @pl.when(index == moment)
            def _(numbers=numbers):
                for number in numbers:
                    packet(number)

        return carry

    lax.fori_loop(0, PARTS, forward, 0)

    passing = neighbour(1)[1]

    def pass_on(index, carry):
        at = quarter(index)
        drain(qg.at[1, :, at, :], far_recv.at[1, index])
        remote(
            qg.at[1, :, at, :], qg.at[3, :, at, :],
            far_send.at[2, index], far_recv.at[3, index], seq=neighbour(0)[0],
        ).start()
        return carry

    drain(delta_in, delta_recv)
    for at in range(lanes):
        rows_of[OWN, 1:2, at * HD : (at + 1) * HD] = delta_in[2 * at] + delta_in[2 * at + 1]
    for slot in range(SLOTS):
        other, inside = neighbour(slot)

        @pl.when(standing(slot)[3])
        def _(slot=slot, other=other):
            pl.semaphore_wait(ready.at[slot], 1)
            if slot != 2:
                for index in range(PARTS):
                    forward_piece(slot, index, other)

        @pl.when(inside)
        def _(slot=slot, other=other):
            there = slot if slot < 2 else 5 - slot
            remote(rows_of.at[OWN], rows_of.at[there], rows_send.at[slot], rows_recv.at[there], seq=other).start()

    def arrive(index):
        at = quarter(index)
        drain(kv.at[:, at, :], kv_recv.at[index])

        @pl.when(index == 0)
        def _():
            for number in range(AFTER[-1][1][-1] + 1, 2 * PARTS):
                packet(number)

        key_t[index] = kv[0, at, :].T

    def item(index, slot):
        at = quarter(index)
        query_rows = qg[slot, 0]
        grad_rows = qg[slot, 1]
        scores = dot(kv[0, at, :], query_rows, NT)
        probs = jnp.exp2(scores * (SCALE * LOG2E) - rows_of[slot, 0:1, :])
        grad_prob = dot(kv[1, at, :], grad_rows, NT)
        probs_low = probs.astype(jnp.bfloat16)
        grad_score = (probs * (grad_prob - rows_of[slot, 1:2, :])).astype(jnp.bfloat16)
        acc_value[at, :] += dot(probs_low, grad_rows, NN)
        acc_key[at, :] += dot(grad_score, query_rows, NN)
        acc_query[slot] += dot(key_t[index], grad_score, NN)

    def far_item(index, slot):
        other, inside = neighbour(slot)

        @pl.when(inside)
        def _():
            @pl.when(index == 0)
            def _():
                drain(rows_of.at[slot], rows_recv.at[slot])
                listed = band[here - other + R, other] == 1
                rows_of[slot, 0:1, :] = jnp.where(listed, rows_of[slot, 0:1, :], UNLISTED)

                @pl.when(slot == 1)
                def _():
                    lax.fori_loop(0, PARTS, pass_on, 0)

                @pl.when(slot != 1)
                def _():
                    for piece in range(PARTS):
                        drain(qg.at[slot, :, pl.ds(piece * chunk, chunk), :], far_recv.at[slot, piece])

            item(index, slot)

            @pl.when(index == PARTS - 1)
            def _():
                there = far_slot(slot)
                for piece in range(PARTS):
                    lanes_of = slice(piece * chunk, (piece + 1) * chunk)
                    term_out[slot, piece] = acc_query[slot, :, lanes_of].astype(jnp.bfloat16)
                    remote(
                        term_out.at[slot, piece], term_in.at[there, piece],
                        term_send.at[slot], term_recv.at[there, piece], seq=other,
                    ).start()

    def send_rows(src, dst, which, place):
        to = sender(place)
        remote(src.at[part(place), :], dst.at[:, cols(head)], res_send.at[which], res_recv.at[which], head=to).start()

    def send_own(src, dst, which):
        pltpu.make_async_copy(src.at[part(0), :], dst.at[:, cols(head)], res_recv.at[which]).start()

    def finish(index):
        at = quarter(index)
        res_kv[0, at, :] = acc_key[at, :].astype(jnp.bfloat16)
        res_kv[1, at, :] = (acc_value[at, :] * (1.0 / SCALE)).astype(jnp.bfloat16)

        def step(place, carry):
            @pl.when(place > 0)
            def _():
                send_rows(res_kv.at[0], out_key, 1, place)
                send_rows(res_kv.at[1], out_value, 2, place)

            return carry

        lax.fori_loop(index * per, index * per + per, step, 0)

    def first_pass(index, carry):
        arrive(index)
        item(index, OWN)

        def step(turn, carry):
            far_item(index, ordered(turn))
            return carry

        return lax.fori_loop(0, near, step, carry)

    def whole_pass(turn, carry):
        def step(index, carry):
            far_item(index, ordered(turn))
            return carry

        return lax.fori_loop(0, PARTS, step, carry)

    def second_pass(index, carry):
        def step(turn, carry):
            far_item(index, ordered(turn))
            return carry

        lax.fori_loop(near + whole, SLOTS, step, 0)
        finish(index)
        return carry

    lax.fori_loop(0, PARTS, first_pass, 0)
    lax.fori_loop(near, near + whole, whole_pass, 0)
    lax.fori_loop(0, PARTS, second_pass, 0)
    send_own(res_kv.at[0], out_key, 1)
    send_own(res_kv.at[1], out_value, 2)

    def query_part(index, carry):
        at = quarter(index)
        acc_part[...] = acc_query[OWN, :, at]
        for slot in range(SLOTS):

            @pl.when(neighbour(slot)[1])
            def _(slot=slot):
                drain(term_in.at[slot, index], term_recv.at[slot, index])
                acc_part[...] += term_in[slot, index].astype(jnp.float32)

        res_query[at, :] = acc_part[...].T.astype(jnp.bfloat16)

        def step(place, carry):
            @pl.when(place > 0)
            def _():
                send_rows(res_query, out_query, 0, place)

            return carry

        lax.fori_loop(index * per, index * per + per, step, 0)
        return carry

    lax.fori_loop(0, PARTS, query_part, 0)
    send_own(res_query, out_query, 0)

    sent = pl.ds(0, (nhead - 1) * rows)
    drain(qg.at[OWN, :, sent, :], qg_send)
    drain(kv.at[:, sent, :], kv_send)
    drain(delta_in.at[pl.ds(0, nhead - 1)], delta_send)
    for slot in range(SLOTS):
        inside = neighbour(slot)[1]

        @pl.when(passing if slot == 2 else inside)
        def _(slot=slot):
            for piece in range(PARTS):
                drain(qg.at[OWN, :, pl.ds(piece * chunk, chunk), :], far_send.at[slot, piece])

        @pl.when(inside)
        def _(slot=slot):
            drain(rows_of.at[OWN], rows_send.at[slot])
            drain(term_out.at[slot], term_send.at[slot])

    for which in range(3):
        drain(res_query.at[sent, :], res_send.at[which])
    drain(out_key, res_recv.at[1])
    drain(out_value, res_recv.at[2])
    drain(out_query, res_recv.at[0])


def per_device(query, key, value, attn_out, grad_out, lse, band):
    nseq, nhead = lax.axis_size("seq"), lax.axis_size("head")
    rows, width = query.shape
    block = rows * nhead
    low, full = jnp.bfloat16, jnp.float32
    vmem = pl.BlockSpec(memory_space=pltpu.VMEM)
    hbm = pl.BlockSpec(memory_space=pltpu.HBM)
    dma = pltpu.SemaphoreType.DMA

    def body(*refs):
        kernel(nseq, nhead, *refs)

    return pl.pallas_call(
        body,
        out_shape=(pltpu.VMEM((rows, width), low),) * 3,
        in_specs=[hbm] * 6 + [pl.BlockSpec(memory_space=pltpu.SMEM)],
        out_specs=[vmem] * 3,
        scratch_shapes=[pltpu.VMEM((rows, width), low)] * 5
        + [
            pltpu.VMEM((1, block), full),
            pltpu.VMEM((block // HD, HD), full),
            pltpu.VMEM((HD, HD), full),
            pltpu.VMEM((SLOTS + 1, 2, block, HD), low),
            pltpu.VMEM((2, block, HD), low),
            pltpu.VMEM((SLOTS + 1, 2, block), full),
            pltpu.VMEM((nhead, 1, HD), full),
            pltpu.VMEM((nhead, 1, HD), full),
            pltpu.VMEM((PARTS, HD, block // PARTS), low),
            pltpu.VMEM((SLOTS + 1, HD, block), full),
            pltpu.VMEM((HD, block // PARTS), full),
            pltpu.VMEM((block, HD), full),
            pltpu.VMEM((block, HD), full),
            pltpu.VMEM((SLOTS, PARTS, HD, block // PARTS), low),
            pltpu.VMEM((SLOTS, PARTS, HD, block // PARTS), low),
            pltpu.VMEM((block, HD), low),
            pltpu.VMEM((2, block, HD), low),
            dma((6,)),
            dma, dma((PARTS,)), dma, dma((PARTS,)), dma, dma,
            dma((SLOTS, PARTS)), dma((SLOTS, PARTS)),
            dma((SLOTS,)), dma((SLOTS,)),
            dma((SLOTS,)), dma((SLOTS, PARTS)),
            dma((3,)), dma((3,)),
            pltpu.SemaphoreType.REGULAR((SLOTS,)),
        ],
        compiler_params=pltpu.CompilerParams(
            collective_id=0, has_side_effects=True, vmem_limit_bytes=62 * 2**20
        ),
        cost_estimate=pl.CostEstimate(
            flops=25 * 2 * block * block * HD, bytes_accessed=8 * rows * width * 2,
            transcendentals=5 * block * block,
        ),
        name="attention_grads",
    )(query, key, value, attn_out, grad_out, lse, band.T)


def solution(mesh):
    rows = P(("seq", "head"), None)
    return jax.shard_map(
        per_device, mesh=mesh, in_specs=(rows,) * 5 + (P("head", "seq"), P()),
        out_specs=(rows,) * 3, check_vma=False,
    )
```

```python
import math

import jax
import jax.numpy as jnp
from jax import lax
from jax.experimental import pallas as pl
from jax.experimental.pallas import tpu as pltpu
from jax.sharding import PartitionSpec as P

R = 2
HD = 128
SLOTS = 2 * R
OWN = SLOTS
PARTS = 4
FIRST = 4
AFTER = ((1, (4,)), (2, (5,)), (3, (6,)))
LOG2E = 1.4426950408889634
SCALE = 1.0 / math.sqrt(HD)
UNLISTED = 1e30
MESH = pl.DeviceIdType.MESH
NT = (((1,), (1,)), ((), ()))
NN = (((1,), (0,)), ((), ()))


def dot(a, b, dims):
    return lax.dot_general(a, b, dims, preferred_element_type=jnp.float32)


def slot_step(slot, sign):
    return sign * (1 + slot // 2) * (1 - 2 * ((slot * (3 - slot)) // 2))


def far_slot(slot):
    return jnp.where(slot < 2, slot, 5 - slot)


def kernel(
    nseq,
    nhead,
    query_hbm,
    key_hbm,
    value_hbm,
    attn_out_hbm,
    grad_out_hbm,
    lse_hbm,
    band,
    out_query,
    out_key,
    out_value,
    query,
    key,
    value,
    attn_out,
    grad_out,
    lse,
    lse_rows,
    across,
    qg,
    kv,
    rows_of,
    delta_out,
    delta_in,
    key_t,
    acc_query,
    acc_part,
    acc_key,
    acc_value,
    term_out,
    term_in,
    res_query,
    res_kv,
    load_sem,
    qg_send,
    qg_recv,
    kv_send,
    kv_recv,
    delta_send,
    delta_recv,
    far_send,
    far_recv,
    rows_send,
    rows_recv,
    term_send,
    term_recv,
    res_send,
    res_recv,
    ready,
):
    here = lax.axis_index("seq")
    head = lax.axis_index("head")
    sign = 1 - 2 * lax.rem(here, 2)
    row = nseq // 2 if nseq >= 8 * R else nseq
    place_in_row = lax.rem(here, row)
    at_end = jnp.logical_or(place_in_row == 0, place_in_row == row - 1)
    beside_end = jnp.logical_or(place_in_row == 1, place_in_row == row - 2)
    rows = query.shape[0]
    block = rows * nhead
    chunk = block // PARTS
    per = nhead // PARTS
    ny = nhead // 2

    def cols(which):
        return pl.ds(pl.multiple_of(which * HD, HD), HD)

    def part(which):
        return pl.ds(pl.multiple_of(which * rows, rows), rows)

    def quarter(which):
        return pl.ds(pl.multiple_of(which * chunk, chunk), chunk)

    def offset(place):
        if ny != 8:
            return place // 2, place % 2
        group, which = place // 4, place % 4
        reach = jnp.where(group == 3, 2, 1 + 2 * (which // 2))
        along_y = jnp.where(which % 2 == 1, ny - reach, reach)
        along_y = jnp.where(group == 0, 4 * (which // 2), along_y)
        along_x = jnp.where(group == 0, which % 2, jnp.where(group == 3, which // 2, group - 1))
        return along_y, along_x

    def sender(place):
        along_y, along_x = offset(place)
        return 2 * lax.rem(head // 2 + ny - along_y, ny) + lax.rem(head + along_x, 2)

    def receiver(place):
        along_y, along_x = offset(place)
        return 2 * lax.rem(head // 2 + along_y, ny) + lax.rem(head + along_x, 2)

    def after(step):
        return lax.rem(head + step, nhead)

    def neighbour(slot):
        other = here + slot_step(slot, sign)
        return other, jnp.logical_and(other >= 0, other < nseq)

    def standing(slot):
        other, inside = neighbour(slot)
        ahead = lax.rem(other + nseq, row) - place_in_row
        later = jnp.logical_and(inside, ahead > 0)
        earlier = jnp.logical_and(inside, ahead < 0)
        return other, later, earlier, jnp.logical_and(inside, ahead > R)

    def ordered(turn):
        early_last = jnp.where(turn == 1, 3, jnp.where(turn > 1, turn - 1, 0))
        late_first = jnp.where(turn > 1, 5 - turn, turn)
        slot = jnp.where(place_in_row == 0, early_last, turn)
        return jnp.where(place_in_row == row - 2, late_first, slot)

    near = jnp.where(at_end, 1, 2)
    whole = jnp.where(jnp.logical_or(at_end, beside_end), 1, 0)

    def remote(src, dst, send, recv, **where):
        return pltpu.make_async_remote_copy(
            src_ref=src, dst_ref=dst, send_sem=send, recv_sem=recv,
            device_id=where, device_id_type=MESH,
        )

    def drain(ref, sem):
        pltpu.make_async_copy(ref, ref, sem).wait()

    loads = [
        pltpu.make_async_copy(src, dst, load_sem.at[at])
        for at, (src, dst) in enumerate(
            (
                (query_hbm, query),
                (grad_out_hbm, grad_out),
                (attn_out_hbm, attn_out),
                (key_hbm, key),
                (value_hbm, value),
                (lse_hbm, lse),
            )
        )
    ]
    for load in loads:
        load.start()

    barrier = pltpu.get_barrier_semaphore()

    def greet(step, carry):
        pl.semaphore_signal(barrier, inc=1, device_id={"head": after(step)}, device_id_type=MESH)
        return carry

    lax.fori_loop(1, nhead, greet, 0)
    count = nhead - 1
    for slot in range(SLOTS):
        other, later, earlier, _ = standing(slot)
        count = count + jnp.where(earlier, 1, 0)

        @pl.when(later)
        def _(other=other):
            pl.semaphore_signal(barrier, inc=1, device_id={"seq": other}, device_id_type=MESH)

    pl.semaphore_wait(barrier, count)
    for slot in range(SLOTS):
        other, _, earlier, _ = standing(slot)

        @pl.when(earlier)
        def _(slot=slot, other=other):
            there = slot if slot < 2 else 5 - slot
            pl.semaphore_signal(ready.at[there], inc=1, device_id={"seq": other}, device_id_type=MESH)

    def exchange(first, second, dst, send, recv, index):
        def step(place, carry):
            to = receiver(place)

            @pl.when(place > 0)
            def _():
                remote(first.at[:, cols(to)], dst.at[0, part(place), :], send, recv.at[index], head=to).start()
                remote(second.at[:, cols(to)], dst.at[1, part(place), :], send, recv.at[index], head=to).start()

            return carry

        lax.fori_loop(index * per, index * per + per, step, 0)

    def packet(number):
        if number < PARTS:
            exchange(query, grad_out, qg.at[OWN], qg_send, qg_recv, number)
        else:
            exchange(key, value, kv, kv_send, kv_recv, number - PARTS)

    for load in loads[:2] + loads[3:5]:
        load.wait()
    for number in range(FIRST):
        packet(number)
    for at, (first, second) in enumerate(((query, grad_out), (key, value))):
        dst, recv = ((qg.at[OWN], qg_recv), (kv, kv_recv))[at]
        pltpu.make_async_copy(first.at[:, cols(head)], dst.at[0, part(0), :], recv.at[0]).start()
        pltpu.make_async_copy(second.at[:, cols(head)], dst.at[1, part(0), :], recv.at[0]).start()

    loads[2].wait()
    lane = lax.broadcasted_iota(jnp.int32, (rows, HD), 1)
    sums = jnp.zeros((rows, HD), jnp.float32)
    for which in range(nhead):
        at = slice(which * HD, (which + 1) * HD)
        product = grad_out[:, at].astype(jnp.float32) * attn_out[:, at].astype(jnp.float32)
        sums = jnp.where(lane == which, jnp.sum(product, axis=1, keepdims=True), sums)
    across[...] = jnp.concatenate([sums, sums], axis=0).T
    low_half = lax.broadcasted_iota(jnp.int32, (1, HD), 1) < rows
    for place in range(nhead):
        to = receiver(place)
        mine = low_half if place % 2 == 0 else jnp.logical_not(low_half)
        delta_out[place] = jnp.where(mine, across[pl.ds(to, 1), :], 0.0)
        if place:
            remote(delta_out.at[place], delta_in.at[place], delta_send, delta_recv, head=to).start()
        else:
            pltpu.make_async_copy(delta_out.at[0], delta_in.at[0], delta_recv).start()

    loads[5].wait()
    lanes = block // HD
    for at in range(lanes):
        lse_rows[at : at + 1, :] = lse[:, at * HD : (at + 1) * HD]

    def lse_half(place):
        source = sender(place)
        one = lse_rows[pl.ds(source // 2, 1), :]
        other = jnp.concatenate([one[:, rows:], one[:, :rows]], axis=1)
        return jnp.where(lax.rem(source, 2) == place % 2, one, other)

    for at in range(lanes):
        turned = jnp.where(low_half, lse_half(2 * at), lse_half(2 * at + 1))
        rows_of[OWN, 0:1, at * HD : (at + 1) * HD] = turned * LOG2E + math.log2(1.0 / SCALE)
    acc_query[...] = jnp.zeros_like(acc_query)
    acc_key[...] = jnp.zeros_like(acc_key)
    acc_value[...] = jnp.zeros_like(acc_value)

    def forward_piece(slot, index, other):
        there = slot if slot < 2 else 5 - slot
        at = quarter(index)
        remote(
            qg.at[OWN, :, at, :], qg.at[there, :, at, :],
            far_send.at[slot, index], far_recv.at[there, index], seq=other,
        ).start()

    def forward(index, carry):
        drain(qg.at[OWN, :, quarter(index), :], qg_recv.at[index])
        for slot in range(SLOTS):
            other, later, earlier, late = standing(slot)
            prompt = jnp.logical_and(later, jnp.logical_not(late))
            @pl.when(prompt)
            def _(slot=slot, other=other):
                @pl.when(index == 0)
                def _():
                    pl.semaphore_wait(ready.at[slot], 1)

                if slot != 2:
                    forward_piece(slot, index, other)

            @pl.when(jnp.logical_and(earlier, slot != 2))
            def _(slot=slot, other=other):
                forward_piece(slot, index, other)

        for moment, numbers in AFTER:

            @pl.when(index == moment)
            def _(numbers=numbers):
                for number in numbers:
                    packet(number)

        return carry

    lax.fori_loop(0, PARTS, forward, 0)

    passing = neighbour(1)[1]

    def pass_on(index, carry):
        at = quarter(index)
        drain(qg.at[1, :, at, :], far_recv.at[1, index])
        remote(
            qg.at[1, :, at, :], qg.at[3, :, at, :],
            far_send.at[2, index], far_recv.at[3, index], seq=neighbour(0)[0],
        ).start()
        return carry

    drain(delta_in, delta_recv)
    for at in range(lanes):
        rows_of[OWN, 1:2, at * HD : (at + 1) * HD] = delta_in[2 * at] + delta_in[2 * at + 1]
    for slot in range(SLOTS):
        other, inside = neighbour(slot)

        @pl.when(standing(slot)[3])
        def _(slot=slot, other=other):
            pl.semaphore_wait(ready.at[slot], 1)
            if slot != 2:
                for index in range(PARTS):
                    forward_piece(slot, index, other)

        @pl.when(inside)
        def _(slot=slot, other=other):
            there = slot if slot < 2 else 5 - slot
            remote(rows_of.at[OWN], rows_of.at[there], rows_send.at[slot], rows_recv.at[there], seq=other).start()

    def arrive(index):
        at = quarter(index)
        drain(kv.at[:, at, :], kv_recv.at[index])

        @pl.when(index == 0)
        def _():
            for number in range(AFTER[-1][1][-1] + 1, 2 * PARTS):
                packet(number)

        key_t[index] = kv[0, at, :].T

    def item(index, slot):
        at = quarter(index)
        query_rows = qg[slot, 0]
        grad_rows = qg[slot, 1]
        scores = dot(kv[0, at, :], query_rows, NT)
        probs = jnp.exp2(scores * (SCALE * LOG2E) - rows_of[slot, 0:1, :])
        grad_prob = dot(kv[1, at, :], grad_rows, NT)
        probs_low = probs.astype(jnp.bfloat16)
        grad_score = (probs * (grad_prob - rows_of[slot, 1:2, :])).astype(jnp.bfloat16)
        acc_value[at, :] += dot(probs_low, grad_rows, NN)
        acc_key[at, :] += dot(grad_score, query_rows, NN)
        acc_query[slot] += dot(key_t[index], grad_score, NN)

    def far_item(index, slot):
        other, inside = neighbour(slot)

        @pl.when(inside)
        def _():
            @pl.when(index == 0)
            def _():
                drain(rows_of.at[slot], rows_recv.at[slot])
                listed = band[here - other + R, other] == 1
                rows_of[slot, 0:1, :] = jnp.where(listed, rows_of[slot, 0:1, :], UNLISTED)

                @pl.when(slot == 1)
                def _():
                    lax.fori_loop(0, PARTS, pass_on, 0)

                @pl.when(slot != 1)
                def _():
                    for piece in range(PARTS):
                        drain(qg.at[slot, :, pl.ds(piece * chunk, chunk), :], far_recv.at[slot, piece])

            item(index, slot)

            @pl.when(index == PARTS - 1)
            def _():
                there = far_slot(slot)
                for piece in range(PARTS):
                    lanes_of = slice(piece * chunk, (piece + 1) * chunk)
                    term_out[slot, piece] = acc_query[slot, :, lanes_of].astype(jnp.bfloat16)
                    remote(
                        term_out.at[slot, piece], term_in.at[there, piece],
                        term_send.at[slot], term_recv.at[there, piece], seq=other,
                    ).start()

    def send_rows(src, dst, which, place):
        to = sender(place)
        remote(src.at[part(place), :], dst.at[:, cols(head)], res_send.at[which], res_recv.at[which], head=to).start()

    def send_own(src, dst, which):
        pltpu.make_async_copy(src.at[part(0), :], dst.at[:, cols(head)], res_recv.at[which]).start()

    def finish(index):
        at = quarter(index)
        res_kv[0, at, :] = acc_key[at, :].astype(jnp.bfloat16)
        res_kv[1, at, :] = (acc_value[at, :] * (1.0 / SCALE)).astype(jnp.bfloat16)

        def step(place, carry):
            @pl.when(place > 0)
            def _():
                send_rows(res_kv.at[0], out_key, 1, place)
                send_rows(res_kv.at[1], out_value, 2, place)

            return carry

        lax.fori_loop(index * per, index * per + per, step, 0)

    def first_pass(index, carry):
        arrive(index)
        item(index, OWN)

        def step(turn, carry):
            far_item(index, ordered(turn))
            return carry

        return lax.fori_loop(0, near, step, carry)

    def whole_pass(turn, carry):
        def step(index, carry):
            far_item(index, ordered(turn))
            return carry

        return lax.fori_loop(0, PARTS, step, carry)

    def second_pass(index, carry):
        def step(turn, carry):
            far_item(index, ordered(turn))
            return carry

        lax.fori_loop(near + whole, SLOTS, step, 0)
        finish(index)
        return carry

    lax.fori_loop(0, PARTS, first_pass, 0)
    lax.fori_loop(near, near + whole, whole_pass, 0)
    lax.fori_loop(0, PARTS, second_pass, 0)
    send_own(res_kv.at[0], out_key, 1)
    send_own(res_kv.at[1], out_value, 2)

    def query_part(index, carry):
        at = quarter(index)
        acc_part[...] = acc_query[OWN, :, at]
        for slot in range(SLOTS):

            @pl.when(neighbour(slot)[1])
            def _(slot=slot):
                drain(term_in.at[slot, index], term_recv.at[slot, index])
                acc_part[...] += term_in[slot, index].astype(jnp.float32)

        res_query[at, :] = acc_part[...].T.astype(jnp.bfloat16)

        def step(place, carry):
            @pl.when(place > 0)
            def _():
                send_rows(res_query, out_query, 0, place)

            return carry

        lax.fori_loop(index * per, index * per + per, step, 0)
        return carry

    lax.fori_loop(0, PARTS, query_part, 0)
    send_own(res_query, out_query, 0)

    sent = pl.ds(0, (nhead - 1) * rows)
    drain(qg.at[OWN, :, sent, :], qg_send)
    drain(kv.at[:, sent, :], kv_send)
    drain(delta_in.at[pl.ds(0, nhead - 1)], delta_send)
    for slot in range(SLOTS):
        inside = neighbour(slot)[1]

        @pl.when(passing if slot == 2 else inside)
        def _(slot=slot):
            for piece in range(PARTS):
                drain(qg.at[OWN, :, pl.ds(piece * chunk, chunk), :], far_send.at[slot, piece])

        @pl.when(inside)
        def _(slot=slot):
            drain(rows_of.at[OWN], rows_send.at[slot])
            drain(term_out.at[slot], term_send.at[slot])

    for which in range(3):
        drain(res_query.at[sent, :], res_send.at[which])
    drain(out_key, res_recv.at[1])
    drain(out_value, res_recv.at[2])
    drain(out_query, res_recv.at[0])


def per_device(query, key, value, attn_out, grad_out, lse, band):
    nseq, nhead = lax.axis_size("seq"), lax.axis_size("head")
    rows, width = query.shape
    block = rows * nhead
    low, full = jnp.bfloat16, jnp.float32
    vmem = pl.BlockSpec(memory_space=pltpu.VMEM)
    hbm = pl.BlockSpec(memory_space=pltpu.HBM)
    dma = pltpu.SemaphoreType.DMA

    def body(*refs):
        kernel(nseq, nhead, *refs)

    return pl.pallas_call(
        body,
        out_shape=(pltpu.VMEM((rows, width), low),) * 3,
        in_specs=[hbm] * 6 + [pl.BlockSpec(memory_space=pltpu.SMEM)],
        out_specs=[vmem] * 3,
        scratch_shapes=[pltpu.VMEM((rows, width), low)] * 5
        + [
            pltpu.VMEM((1, block), full),
            pltpu.VMEM((block // HD, HD), full),
            pltpu.VMEM((HD, HD), full),
            pltpu.VMEM((SLOTS + 1, 2, block, HD), low),
            pltpu.VMEM((2, block, HD), low),
            pltpu.VMEM((SLOTS + 1, 2, block), full),
            pltpu.VMEM((nhead, 1, HD), full),
            pltpu.VMEM((nhead, 1, HD), full),
            pltpu.VMEM((PARTS, HD, block // PARTS), low),
            pltpu.VMEM((SLOTS + 1, HD, block), full),
            pltpu.VMEM((HD, block // PARTS), full),
            pltpu.VMEM((block, HD), full),
            pltpu.VMEM((block, HD), full),
            pltpu.VMEM((SLOTS, PARTS, HD, block // PARTS), low),
            pltpu.VMEM((SLOTS, PARTS, HD, block // PARTS), low),
            pltpu.VMEM((block, HD), low),
            pltpu.VMEM((2, block, HD), low),
            dma((6,)),
            dma, dma((PARTS,)), dma, dma((PARTS,)), dma, dma,
            dma((SLOTS, PARTS)), dma((SLOTS, PARTS)),
            dma((SLOTS,)), dma((SLOTS,)),
            dma((SLOTS,)), dma((SLOTS, PARTS)),
            dma((3,)), dma((3,)),
            pltpu.SemaphoreType.REGULAR((SLOTS,)),
        ],
        compiler_params=pltpu.CompilerParams(
            collective_id=0, has_side_effects=True, vmem_limit_bytes=62 * 2**20
        ),
        cost_estimate=pl.CostEstimate(
            flops=25 * 2 * block * block * HD, bytes_accessed=8 * rows * width * 2,
            transcendentals=5 * block * block,
        ),
        name="attention_grads",
    )(query, key, value, attn_out, grad_out, lse, band.T)


def solution(mesh):
    rows = P(("seq", "head"), None)
    return jax.shard_map(
        per_device, mesh=mesh, in_specs=(rows,) * 5 + (P("head", "seq"), P()),
        out_specs=(rows,) * 3, check_vma=False,
    )
```
